512 devices in a mesh: enc: 16 (over x, y_hi, core), seq: 8 (over z), tp: 4 (over y_lo).
Axes of the slice: x: 4, y: 8 (y_hi: 2, y_lo: 4; y = y_hi * 4 + y_lo), z: 8, core: 2. Of those that a mesh axis runs over, the one named last changes fastest.
Arguments:
- patches: bfloat16 [64, 256, 1280], P('enc', 'seq'), may hold values from -1.5 to 1.5
- image_tokens: int32 [16, 4], replicated, may hold values from 1 to 64, 160 in all within a row
- image_gap: int32 [16, 4], replicated, may hold values from 0 to 215
- image_slot: int32 [64], replicated, may hold values from 0 to 63, each once
- norm_gain: float32 [1280], replicated, may hold values from 0.1 to 1.9
- merge_gain: float32 [1280], replicated, may hold values from 0.1 to 1.9
- w_qkv: bfloat16 [1280, 3840], P('enc', 'tp'), may hold values from -0.15625 to 0.15625
- w_out: bfloat16 [1280, 1280], P(('tp', 'enc')), may hold values from -0.625 to 0.625
- kv_merge: bfloat16 [5120, 1024], P('enc', 'tp'), may hold values from -0.078125 to 0.078125
- queries: bfloat16 [16, 1024, 4096], P('enc', 'seq', 'tp'), may hold values from -256 to 256
- text_kv: bfloat16 [16, 1024, 1024], P('enc', 'seq', 'tp'), may hold values from -6 to 6
- cache_kv: bfloat16 [16, 3072, 1024], P('enc', 'seq', 'tp'), may hold values from -6 to 6
Outputs:
- span_attention: bfloat16 [16, 1024, 4096], P('enc', 'seq', 'tp')
The draws below stay inside these ranges and needn't reach their ends.
Inputs may be any that keep to these rules, and one draw needn't show every extreme that they name: `image_tokens`: each row sums to 160, and one image in every prompt has exactly 64 tokens. `image_slot`: a permutation of the slots.
All inputs are finite; a program needn't handle non-finite values.
Results may differ from the reference program's by a relative error of at most 0.017.
Values may be sent and summed in bfloat16 or wider, within the bound.
No kernel may reach another device: no remote copies, remote signals or barrier semaphores. Data moves between devices by JAX's collectives and lax.ppermute only.
A program may use at most 64 MiB of HBM per device.

```python
import math
import jax
import jax.numpy as jnp
import numpy as np
from jax import lax

VD = 1280
VH = 16
VHD = 80
MERGE = 4
QH = 32
KVH = 4
HD = 128
IMG_ENC = 4
SLOT = 256
IMAGES = 64
PROMPTS = 16
SPAN = 1024
CACHE = 3072
IMG_TOTAL = 160
GAP = 216


def cache_base(key):
    values = jax.random.normal(jax.random.fold_in(key, 7), (PROMPTS, CACHE, KVH, 2, HD), jnp.float32)
    return jnp.clip(values, -6.0, 6.0)


def draw_cache_kv(key, part):
    shared = cache_base(key)
    return shared.reshape(PROMPTS, CACHE, KVH * 2 * HD).astype(jnp.bfloat16)


def draw_queries(key, part):
    key = jax.random.fold_in(key, 2)
    base = jnp.clip(jax.random.normal(key, (PROMPTS, SPAN, QH, HD), jnp.float32), -6.0, 6.0)
    return base.reshape(PROMPTS, SPAN, QH * HD).astype(jnp.bfloat16)


def touch_ends(values, own_key, smallest, top_value):
    dims = values.shape
    place = [jax.random.randint(jax.random.fold_in(own_key, axis), (), 0, dims[axis]) for axis in range(len(dims))]
    values = values.at[tuple(place)].set(smallest)
    longest = dims.index(max(dims))
    place[longest] = (place[longest] + 1) % dims[longest]
    return values.at[tuple(place)].set(top_value)


def levels(stream_key, extent, shards, least, top_value):
    def one(dim, parts):
        draws = jax.random.uniform(jax.random.fold_in(jax.random.fold_in(stream_key, 6), dim), (parts,), jnp.float32, least / len(shards), top_value / len(shards))
        return jnp.repeat(jnp.exp(draws), extent[dim] // parts).reshape((-1,) + (1,) * (len(extent) - dim - 1))

    level = one(*shards[0])
    for cut in shards[1:]:
        level = level * one(*cut)
    return level


def length_profile(amount, total, most, skew):
    portions = [(1 << 20) // math.isqrt(grade ** skew) + 1 for grade in range(2, amount + 1)]
    spare, holding = total - most - (amount - 1), [1] * (amount - 1)
    while spare > 0:
        movable = [i for i in range(amount - 1) if holding[i] < most]
        pool, left = sum([portions[i] for i in movable]), spare
        for i in movable:
            more = min(most - holding[i], max(1, left * portions[i] // pool), spare)
            holding[i] = holding[i] + more
            spare = spare - more
    return np.array([most] + holding)


def ragged_sizes(key, amount, total, bound, skew):
    if amount == 2:
        one = jax.random.randint(key, (), max(1, total - bound), min(bound, total - 1) + 1)
        return jnp.stack([one, total - one])
    sizes = jnp.asarray(length_profile(amount, total, bound, skew), jnp.int32)
    twos = (amount - 1) // 2
    source_of, taker = sizes[1:1 + 2 * twos:2], sizes[2:2 + 2 * twos:2]
    room = jnp.minimum(source_of - 1, bound - taker)
    shifted = jax.random.randint(jax.random.fold_in(key, 1), (twos,), 0, 1 << 20) % (room + 1)
    sizes = sizes.at[1:1 + 2 * twos:2].set(source_of - shifted).at[2:2 + 2 * twos:2].set(taker + shifted)
    return sizes[jax.random.permutation(jax.random.fold_in(key, 2), amount)]


def gaussian(key, shape, scale, most, shards=(), kind=jnp.bfloat16):
    level = levels(key, shape, shards, -0.22, 0.18) if shards else 1.0
    drawn = jax.random.normal(key, shape, jnp.float32) * scale * level
    return jnp.minimum(jnp.maximum(drawn, -most), most).astype(kind)


def setup_inputs(seed: int = 0) -> dict:
    streams_of = jax.random.split(jax.random.key(seed), 13)
    patches = gaussian(streams_of[0], (IMAGES, SLOT, VD), 0.25, 1.5, ((0, 16), (1, 8)))
    image_tokens = jax.vmap(lambda own: ragged_sizes(own, IMG_ENC, IMG_TOTAL, SLOT // MERGE, 2))(jax.random.split(streams_of[1], PROMPTS)).reshape((PROMPTS, IMG_ENC)).astype(jnp.int32)
    image_gap = touch_ends(jax.random.randint(streams_of[2], (PROMPTS, IMG_ENC), 0, GAP), jax.random.fold_in(streams_of[2], 1), 0, GAP - 1).astype(jnp.int32)
    image_slot = jax.random.permutation(streams_of[3], IMAGES).astype(jnp.int32)
    norm_gain = jnp.clip(1.0 + 0.18 * jax.random.normal(streams_of[4], (VD,), jnp.float32), 0.1, 1.9)
    merge_gain = jnp.clip(1.0 + 0.18 * jax.random.normal(streams_of[5], (VD,), jnp.float32), 0.1, 1.9)
    w_qkv = gaussian(streams_of[6], (VD, VH * 3 * VHD), VD ** -0.5, 0.15625, ((0, 16), (1, 4)))
    w_out = gaussian(streams_of[7], (VH * VHD, VD), (VH * VHD // 16) ** -0.5, 0.625, ((0, 64),))
    kv_merge = gaussian(streams_of[8], (MERGE * VD, KVH * 2 * HD), (MERGE * VD) ** -0.5, 0.078125, ((0, 16), (1, 4)))
    queries = draw_queries(jax.random.fold_in(streams_of[12], 71), 0)
    text_kv = gaussian(streams_of[10], (PROMPTS, SPAN, KVH * 2 * HD), 1.0, 6.0, ((0, 16), (1, 8), (2, 4)))
    cache_kv = draw_cache_kv(jax.random.fold_in(streams_of[12], 71), 0)
    return dict(patches=patches, image_tokens=image_tokens, image_gap=image_gap, image_slot=image_slot, norm_gain=norm_gain, merge_gain=merge_gain, w_qkv=w_qkv, w_out=w_out, kv_merge=kv_merge, queries=queries, text_kv=text_kv, cache_kv=cache_kv)


EPS = 1e-06
FAR = 1 << 30
NEG = -1e+30

def rms_scale(values, gain):
    return values * lax.rsqrt(lax.optimization_barrier(jnp.mean(values * values, axis=-1, keepdims=True)) + EPS) * gain.astype(jnp.float32)

def reference(patches, image_tokens, image_gap, image_slot, norm_gain, merge_gain, w_qkv, w_out, kv_merge, queries, text_kv, cache_kv):
    counts_flat = image_tokens.reshape(-1).astype(jnp.int32)
    slot_count = jnp.zeros((IMAGES,), jnp.int32).at[image_slot].set(counts_flat)

    def encode(packed):
        slot_patch, image_count = packed
        source = slot_patch.astype(jnp.float32)
        normed = rms_scale(source, norm_gain).astype(jnp.bfloat16)
        qkv_rows = jnp.dot(normed, w_qkv, preferred_element_type=jnp.float32).astype(jnp.bfloat16)
        qkv_rows = qkv_rows.reshape(SLOT, VH, 3, VHD).astype(jnp.float32)
        scores = jnp.einsum('qhd,khd->hqk', qkv_rows[:, :, 0], qkv_rows[:, :, 1]) / math.sqrt(VHD)
        visible = jnp.arange(SLOT, dtype=jnp.int32) < MERGE * image_count
        scores = jnp.where(visible[None, None, :], scores, NEG)
        weights = jax.nn.softmax(scores, axis=-1).astype(jnp.bfloat16)
        attended = jnp.einsum('hqk,khd->qhd', weights.astype(jnp.float32), qkv_rows[:, :, 2])
        attended = attended.astype(jnp.bfloat16).reshape(SLOT, VH * VHD)
        residual = source + jnp.dot(attended, w_out, preferred_element_type=jnp.float32)
        merged = rms_scale(residual, merge_gain).astype(jnp.bfloat16).reshape(SLOT // MERGE, MERGE * VD)
        return jnp.dot(merged, kv_merge, preferred_element_type=jnp.float32).astype(jnp.bfloat16)
    image_kv = lax.map(encode, (patches, slot_count))
    starts = (jnp.cumsum(image_gap, axis=-1) + jnp.cumsum(image_tokens, axis=-1) - image_tokens).astype(jnp.int32)
    group_size = QH // KVH
    positions = jnp.arange(SPAN, dtype=jnp.int32)
    token_index = jnp.arange(SLOT // MERGE, dtype=jnp.int32)

    def prompt_attention(prompt):
        image_begin = starts[prompt]
        image_count = image_tokens[prompt].astype(jnp.int32)
        my_slots = lax.dynamic_slice_in_dim(image_slot, prompt * IMG_ENC, IMG_ENC)
        images = image_kv[my_slots].reshape(IMG_ENC * (SLOT // MERGE), KVH * 2 * HD)
        inside = jnp.any((positions[None, :] >= image_begin[:, None]) & (positions[None, :] < (image_begin + image_count)[:, None]), axis=0)
        text_pos = jnp.where(inside, FAR, positions).astype(jnp.int32)
        image_pos = jnp.where(token_index[None, :] < image_count[:, None], image_begin[:, None] + token_index[None, :], FAR).reshape(-1).astype(jnp.int32)
        key_pos = jnp.concatenate([jnp.full((CACHE,), -1, jnp.int32), text_pos, image_pos])
        all_keys = jnp.concatenate([cache_kv[prompt], text_kv[prompt], images], axis=0).reshape(-1, KVH, 2, HD)
        visible = key_pos[None, :] <= positions[:, None]
        query_rows = queries[prompt].reshape(SPAN, QH, HD)

        def one_head(head_index):
            keys_head = lax.dynamic_index_in_dim(all_keys, head_index // group_size, 1, keepdims=False)
            query_head = lax.dynamic_index_in_dim(query_rows, head_index, 1, keepdims=False)
            scores = jnp.dot(query_head, keys_head[:, 0].T, preferred_element_type=jnp.float32) / math.sqrt(HD)
            scores = jnp.where(visible, scores, NEG)
            weights = jax.nn.softmax(scores, axis=-1).astype(jnp.bfloat16)
            return jnp.dot(weights, keys_head[:, 1], preferred_element_type=jnp.float32).astype(jnp.bfloat16)
        per_head = lax.map(one_head, jnp.arange(QH, dtype=jnp.int32))
        return jnp.transpose(per_head, (1, 0, 2)).reshape(SPAN, QH * HD)
    return lax.map(prompt_attention, jnp.arange(PROMPTS, dtype=jnp.int32))
```

```python
import math

import jax
import jax.numpy as jnp
from jax import lax
from jax.experimental import pallas as pl
from jax.experimental.pallas import tpu as pltpu
from jax.sharding import Mesh
from jax.sharding import PartitionSpec as P

VD = 1280
VHD = 80
MERGE = 4
HD = 128
GROUP = 8
IMG_ENC = 4
SLOT = 256
TOK = SLOT // MERGE
IMG_TOTAL = 160
SPAN = 1024
CACHE = 3072

EPS = 1e-06
FAR = 1 << 30
NEG = -1e30
LOG2E = math.log2(math.e)

ENC = ("x", "yh", "core")
SEQ = ("j", "h")
VMEM = pl.BlockSpec(memory_space=pltpu.VMEM)
SMEM = pl.BlockSpec(memory_space=pltpu.SMEM)
ANY = pl.BlockSpec(memory_space=pl.ANY)


def params(mib=48):
    return pltpu.CompilerParams(vmem_limit_bytes=mib << 20)


def swap(value, axis):
    return lax.ppermute(value, axis, [(0, 1), (1, 0)])


def rms_scale(values, gain):
    return values * lax.rsqrt(jnp.mean(values * values, axis=-1, keepdims=True) + EPS) * gain


def vision_kernel(ids, tokens, slots, patches, gain, own, other, out, weight):
    core, slot = ids[2], ids[3]
    for piece in range(8):
        weight[pl.ds(pl.multiple_of((piece * 2 + core) * 80, 16), 80), 0:480] = own[piece]
        weight[pl.ds(pl.multiple_of((piece * 2 + 1 - core) * 80, 16), 80), 0:480] = other[piece]
    count = jnp.int32(0)
    for i in range(slots.shape[0]):
        count = jnp.where(slots[i] == slot, tokens[i // IMG_ENC, i % IMG_ENC], count)
    rows = patches[...].reshape(SLOT, VD).astype(jnp.float32)
    normed = rms_scale(rows, gain[...]).astype(jnp.bfloat16)
    qkv = jnp.dot(normed, weight[...], preferred_element_type=jnp.float32)
    flipped = jnp.transpose(qkv).astype(jnp.bfloat16)
    live = lax.broadcasted_iota(jnp.int32, (SLOT, SLOT), 0) < MERGE * count
    for head in range(2):
        base = head * 3 * VHD
        keys = qkv[:, base + VHD : base + 2 * VHD].astype(jnp.bfloat16)
        scores = jnp.dot(
            keys, flipped[base : base + VHD], preferred_element_type=jnp.float32
        ) * (1.0 / math.sqrt(VHD))
        scores = jnp.where(live, scores, NEG)
        weights = jnp.exp(scores - jnp.max(scores, axis=0, keepdims=True))
        denom = jnp.sum(weights, axis=0, keepdims=True)
        attended = jnp.dot(
            flipped[base + 2 * VHD : base + 3 * VHD],
            weights.astype(jnp.bfloat16),
            preferred_element_type=jnp.float32,
        )
        attended = (attended / denom).astype(jnp.bfloat16)
        for peer in range(out.shape[0]):
            out[peer, head * VHD : (head + 1) * VHD, :] = attended


def merge_kernel(attended, w_out, patches, gain, kv_merge, out, merged):
    residual = patches[...].reshape(SLOT, VD).astype(jnp.float32) + lax.dot_general(
        attended[...].reshape(VD, SLOT),
        w_out[...],
        (((0,), (0,)), ((), ())),
        preferred_element_type=jnp.float32,
    )
    residual = rms_scale(residual, gain[...])
    for c in range(VD // 128):
        merged[c] = residual[:, c * 128 : (c + 1) * 128]
    total = jnp.zeros((TOK, HD), jnp.float32)
    for r in range(MERGE):
        part = [merged[c, pl.ds(r, TOK, stride=MERGE), :] for c in range(VD // 128)]
        part = jnp.concatenate(part, axis=1).astype(jnp.bfloat16)
        total += jnp.dot(
            part, kv_merge[r * VD : (r + 1) * VD, :], preferred_element_type=jnp.float32
        )
    total = total.astype(jnp.bfloat16)
    for peer in range(out.shape[0]):
        out[peer] = total


def select_kernel(ids, tokens, slots, images, out):
    prompt, plane = ids[0], ids[1]
    shape = (IMG_TOTAL, images.shape[0] * TOK)
    row = lax.broadcasted_iota(jnp.int32, shape, 0)
    column = lax.broadcasted_iota(jnp.int32, shape, 1)
    wanted = jnp.full(shape, -1, jnp.int32)
    begin = jnp.int32(0)
    for k in range(IMG_ENC):
        slot = slots[prompt * IMG_ENC + k]
        count = tokens[prompt, k]
        base = jnp.where(slot % IMG_ENC == plane, (slot // IMG_ENC) * TOK - begin, -FAR)
        inside = (row >= begin) & (row < begin + count)
        wanted = jnp.where(inside, row + base, wanted)
        begin = begin + count
    selector = (column == wanted).astype(jnp.bfloat16)
    packed = jnp.dot(
        selector, images[...].reshape(shape[1], HD), preferred_element_type=jnp.float32
    ).astype(jnp.bfloat16)
    for peer in range(out.shape[0]):
        out[peer] = packed


def stack_queries(queries, stacked):
    for g in range(GROUP):
        stacked[g * 128 : (g + 1) * 128, :] = queries[0, :, g * HD : (g + 1) * HD]


def text_kernel(ids, tokens, gaps, queries, cached, after, out, top_out, sum_out, stacked, top, accum):
    del after
    prompt, seq = ids[0], ids[4]
    stack_queries(queries, stacked)
    rows = GROUP * 128
    factor = LOG2E / math.sqrt(HD)
    begin = jnp.int32(0)
    spans = []
    for k in range(IMG_ENC):
        begin = begin + gaps[prompt, k]
        spans.append((begin, begin + tokens[prompt, k]))
        begin = begin + tokens[prompt, k]
    top[...] = jnp.full((rows, 1), NEG, jnp.float32)
    accum[...] = jnp.zeros((rows, HD), jnp.float32)
    total = jnp.zeros((rows, 1), jnp.float32)

    def block(keys, values, visible, total):
        scores = lax.dot_general(
            stacked[...], keys, (((1,), (1,)), ((), ())), preferred_element_type=jnp.float32
        )
        if visible is not None:
            scores = jnp.where(visible, scores, NEG)
        highest = jnp.maximum(top[...], jnp.max(scores, axis=-1, keepdims=True))
        scale = jnp.exp2((top[...] - highest) * factor)
        weights = jnp.exp2((scores - highest) * factor)
        top[...] = highest
        accum[...] = accum[...] * scale + jnp.dot(
            weights.astype(jnp.bfloat16), values, preferred_element_type=jnp.float32
        )
        return total * scale + jnp.sum(weights, axis=-1, keepdims=True)

    for z in range(8):
        total = block(cached[z, 0:384, 0:HD], cached[z, 0:384, HD:], None, total)
    for part in range(4):
        base = part * 256
        position = base + lax.broadcasted_iota(jnp.int32, (1, 256), 1)
        for low, high in spans:
            inside = (position >= low) & (position < high)
            position = jnp.where(inside, FAR, position)
        query = seq * 128 + lax.broadcasted_iota(jnp.int32, (rows, 1), 0) % 128
        keys = cached[2 * part : 2 * part + 2, 384:512, 0:HD].reshape(256, HD)
        values = cached[2 * part : 2 * part + 2, 384:512, HD:].reshape(256, HD)
        total = block(keys, values, position <= query, total)
    out[...] = accum[...]
    top_out[...] = top[...]
    sum_out[...] = total


def join_kernel(ids, tokens, gaps, queries, images, accum, top, total, out, stacked):
    prompt, seq = ids[0], ids[4]
    stack_queries(queries, stacked)
    rows = GROUP * 128
    factor = LOG2E / math.sqrt(HD)
    keys = (images[0] + images[2]) + (images[4] + images[6])
    values = (images[1] + images[3]) + (images[5] + images[7])
    index = lax.broadcasted_iota(jnp.int32, (1, IMG_TOTAL), 1)
    position = jnp.full((1, IMG_TOTAL), FAR, jnp.int32)
    shift = jnp.int32(0)
    begin = jnp.int32(0)
    for k in range(IMG_ENC):
        shift = shift + gaps[prompt, k]
        position = jnp.where(index >= begin, index + shift, position)
        begin = begin + tokens[prompt, k]
    query = seq * 128 + lax.broadcasted_iota(jnp.int32, (rows, 1), 0) % 128
    scores = lax.dot_general(
        stacked[...], keys, (((1,), (1,)), ((), ())), preferred_element_type=jnp.float32
    )
    scores = jnp.where(position <= query, scores, NEG)
    highest = jnp.maximum(top[...], jnp.max(scores, axis=-1, keepdims=True))
    scale = jnp.exp2((top[...] - highest) * factor)
    weights = jnp.exp2((scores - highest) * factor)
    denom = total[...] * scale + jnp.sum(weights, axis=-1, keepdims=True)
    joined = accum[...] * scale + jnp.dot(
        weights.astype(jnp.bfloat16), values, preferred_element_type=jnp.float32
    )
    joined = (joined / denom).astype(jnp.bfloat16)
    for g in range(GROUP):
        out[0, :, g * HD : (g + 1) * HD] = joined[g * 128 : (g + 1) * 128, :]


def per_device(
    patches,
    image_tokens,
    image_gap,
    image_slot,
    norm_gain,
    merge_gain,
    w_qkv,
    w_out,
    kv_merge,
    queries,
    text_kv,
    cache_kv,
):
    x, yh, core = (lax.axis_index(a) for a in ENC)
    plane, half = lax.axis_index("j"), lax.axis_index("h")
    enc = (x * 2 + yh) * 2 + core
    ids = jnp.stack([enc, plane, core, enc * IMG_ENC + plane, plane * 2 + half]).astype(jnp.int32)
    bf16, f32 = jnp.bfloat16, jnp.float32

    mine = lax.dynamic_slice_in_dim(w_qkv, half * 480, 480, axis=1)
    both = jnp.stack([mine, swap(mine, "yh")])
    both = jnp.where(yh == 0, both, both[::-1])
    along = lax.all_to_all(jnp.broadcast_to(both[None], (4, 2, 80, 480)), "x", 0, 0)
    own = along.reshape(8, 80, 480)
    other = swap(own, "core")

    sent = jnp.broadcast_to(patches[:, None], (4, 2, 32, VD)).reshape(8, 32, VD)
    image = lax.all_to_all(sent, SEQ, 0, 0)

    group = lax.all_to_all(jnp.broadcast_to(w_out[None], (4, 20, VD)), "tp", 0, 0)
    pair = jnp.stack([group, swap(group, "yh")])
    pair = jnp.where(yh == 0, pair, pair[::-1])
    pair = lax.all_to_all(jnp.broadcast_to(pair[None], (4, 2, 4, 20, VD)), "x", 0, 0)
    cores = jnp.stack([pair, swap(pair, "core")])
    cores = jnp.where(core == 0, cores, cores[::-1])
    out_weight = jnp.transpose(cores, (3, 1, 2, 0, 4, 5)).reshape(VD, VD)

    columns = lax.dynamic_slice_in_dim(kv_merge, half * HD, HD, axis=1)
    merge_weight = lax.all_gather(columns, ENC, axis=0, tiled=True)

    past = jnp.concatenate([cache_kv[0], text_kv[0]], axis=0)
    past = lax.all_to_all(jnp.broadcast_to(past[None], (8, 512, 2 * HD)), SEQ, 0, 0)

    attended = pl.pallas_call(
        vision_kernel,
        out_shape=jax.ShapeDtypeStruct((8, 2 * VHD, SLOT), bf16),
        in_specs=[SMEM] * 3 + [VMEM] * 4,
        out_specs=VMEM,
        scratch_shapes=[pltpu.VMEM((VD, 512), bf16)],
        compiler_params=params(),
        cost_estimate=pl.CostEstimate(flops=400_000_000, bytes_accessed=4_000_000, transcendentals=131072),
        name="vision",
    )(ids, image_tokens, image_slot, image, norm_gain.reshape(1, VD), own, other)
    attended = lax.all_to_all(attended, ("tp", "h"), 0, 0)

    image_kv = pl.pallas_call(
        merge_kernel,
        out_shape=jax.ShapeDtypeStruct((16, TOK, HD), bf16),
        in_specs=[VMEM] * 5,
        out_specs=VMEM,
        scratch_shapes=[pltpu.VMEM((VD // 128, SLOT, 128), f32)],
        compiler_params=params(),
        cost_estimate=pl.CostEstimate(flops=1_000_000_000, bytes_accessed=8_000_000, transcendentals=256),
        name="merge",
    )(attended, out_weight, image, merge_gain.reshape(1, VD), merge_weight)
    every = lax.all_to_all(image_kv, ENC, 0, 0)

    rows = GROUP * 128
    accum, top, total = pl.pallas_call(
        text_kernel,
        out_shape=(
            jax.ShapeDtypeStruct((rows, HD), f32),
            jax.ShapeDtypeStruct((rows, 1), f32),
            jax.ShapeDtypeStruct((rows, 1), f32),
        ),
        in_specs=[SMEM] * 3 + [VMEM] * 2 + [ANY],
        out_specs=(VMEM, VMEM, VMEM),
        scratch_shapes=[
            pltpu.VMEM((rows, HD), bf16),
            pltpu.VMEM((rows, 1), f32),
            pltpu.VMEM((rows, HD), f32),
        ],
        compiler_params=params(),
        cost_estimate=pl.CostEstimate(
            flops=2_200_000_000, bytes_accessed=4_000_000, transcendentals=rows * 4096
        ),
        name="text",
    )(ids, image_tokens, image_gap, queries, past, image_kv)

    packed = pl.pallas_call(
        select_kernel,
        out_shape=jax.ShapeDtypeStruct((8, IMG_TOTAL, HD), bf16),
        in_specs=[SMEM] * 3 + [VMEM],
        out_specs=VMEM,
        compiler_params=params(),
        cost_estimate=pl.CostEstimate(flops=42_000_000, bytes_accessed=600_000, transcendentals=0),
        name="select",
    )(ids, image_tokens, image_slot, every)
    images = lax.all_to_all(packed, SEQ, 0, 0)

    return pl.pallas_call(
        join_kernel,
        out_shape=jax.ShapeDtypeStruct((1, 128, GROUP * HD), bf16),
        in_specs=[SMEM] * 3 + [VMEM] * 5,
        out_specs=VMEM,
        scratch_shapes=[pltpu.VMEM((rows, HD), bf16)],
        compiler_params=params(),
        cost_estimate=pl.CostEstimate(
            flops=84_000_000, bytes_accessed=2_000_000, transcendentals=rows * 160
        ),
        name="join",
    )(ids, image_tokens, image_gap, queries, images, accum, top, total)


def solution(mesh):
    fine = Mesh(
        mesh.devices.reshape(4, 2, 2, 4, 2, 4), ("x", "yh", "core", "j", "h", "tp")
    )
    in_specs = (
        P(ENC, SEQ, None),
        P(),
        P(),
        P(),
        P(),
        P(),
        P(ENC, "tp"),
        P(("tp",) + ENC, None),
        P(ENC, "tp"),
        P(ENC, SEQ, "tp"),
        P(ENC, SEQ, "tp"),
        P(ENC, SEQ, "tp"),
    )
    return jax.shard_map(
        per_device, mesh=fine, in_specs=in_specs, out_specs=P(ENC, SEQ, "tp"), check_vma=False
    )
```

```python
import math

import jax
import jax.numpy as jnp
from jax import lax
from jax.experimental import pallas as pl
from jax.experimental.pallas import tpu as pltpu
from jax.sharding import Mesh
from jax.sharding import PartitionSpec as P

VD = 1280
VHD = 80
MERGE = 4
HD = 128
GROUP = 8
IMG_ENC = 4
SLOT = 256
TOK = SLOT // MERGE
IMG_TOTAL = 160
SPAN = 1024
CACHE = 3072

EPS = 1e-06
FAR = 1 << 30
NEG = -1e30
LOG2E = math.log2(math.e)

ENC = ("x", "yh", "core")
SEQ = ("j", "h")
VMEM = pl.BlockSpec(memory_space=pltpu.VMEM)
SMEM = pl.BlockSpec(memory_space=pltpu.SMEM)
ANY = pl.BlockSpec(memory_space=pl.ANY)


def params(mib=48):
    return pltpu.CompilerParams(vmem_limit_bytes=mib << 20)


def swap(value, axis):
    return lax.ppermute(value, axis, [(0, 1), (1, 0)])


def rms_scale(values, gain):
    return values * lax.rsqrt(jnp.mean(values * values, axis=-1, keepdims=True) + EPS) * gain


def pack_heads_kernel(w_qkv, w_out, out, lines):
    first = jnp.where(lax.axis_index("h") == 0, w_qkv[:, 0:480], w_qkv[:, 480:960])
    for c in range(4):
        size = min(128, 480 - c * 128)
        out[c * 80 : (c + 1) * 80, 0:size] = first[:, c * 128 : c * 128 + size]
    out[240:320, 96:128] = jnp.zeros((80, 32), jnp.bfloat16)
    lines[200:208, :] = jnp.zeros((8, 128), jnp.float32)
    rows = w_out[...].astype(jnp.float32)
    for c in range(10):
        lines[pl.ds(c, 20, stride=10), :] = rows[:, c * 128 : (c + 1) * 128]
    out[320:528, :] = lines[...].astype(jnp.bfloat16)


def pack_merge_kernel(kv_merge, after, out):
    del after
    out[...] = jnp.where(lax.axis_index("h") == 0, kv_merge[:, 0:HD], kv_merge[:, HD:])


def vision_kernel(tokens, slots, patches, gain, own, other, out, weight, lines, rows_out, mixed):
    core, yh, half = lax.axis_index("core"), lax.axis_index("yh"), lax.axis_index("h")
    slot = ((lax.axis_index("x") * 2 + yh) * 2 + core) * IMG_ENC + lax.axis_index("j")
    for x in range(4):
        for rel in range(2):
            for c in range(4):
                base = x * 4 + (yh ^ rel) * 2
                tile = pl.ds(c * 128, 128)
                weight[pl.ds(pl.multiple_of((base + core) * 80, 16), 80), tile] = own[
                    x, rel, c * 80 : (c + 1) * 80, :
                ]
                weight[pl.ds(pl.multiple_of((base + 1 - core) * 80, 16), 80), tile] = other[
                    x, rel, c * 80 : (c + 1) * 80, :
                ]
    rows_out[...] = jnp.zeros(rows_out.shape, jnp.float32)
    for head in range(2):
        for rel in range(2):
            for part, piece in enumerate((own, other)):
                base = head * 128 + (rel * 2 + part) * 32
                lines[...] = piece[half * 2 + head, rel, 320:528, :].astype(jnp.float32)
                for c in range(10):
                    rows_out[base : base + 20, c * 128 : (c + 1) * 128] = lines[
                        pl.ds(c, 20, stride=10), :
                    ]
    row = lax.broadcasted_iota(jnp.int32, (128, VHD), 0)
    column = lax.broadcasted_iota(jnp.int32, (128, VHD), 1)
    wanted = ((row // 32) ^ (yh * 2 + core)) * 20 + row % 32
    order = ((column == wanted) & (row % 32 < 20)).astype(jnp.bfloat16)
    count = jnp.int32(0)
    for i in range(slots.shape[0]):
        count = jnp.where(slots[i] == slot, tokens[i // IMG_ENC, i % IMG_ENC], count)
    rows = patches[...].reshape(SLOT, VD).astype(jnp.float32)
    normed = rms_scale(rows, gain[...]).astype(jnp.bfloat16)
    qkv = jnp.dot(normed, weight[...], preferred_element_type=jnp.float32)
    flipped = jnp.transpose(qkv).astype(jnp.bfloat16)
    live = lax.broadcasted_iota(jnp.int32, (SLOT, SLOT), 0) < MERGE * count
    for head in range(2):
        base = head * 3 * VHD
        keys = qkv[:, base + VHD : base + 2 * VHD].astype(jnp.bfloat16)
        scores = jnp.dot(
            keys, flipped[base : base + VHD], preferred_element_type=jnp.float32
        ) * (1.0 / math.sqrt(VHD))
        scores = jnp.where(live, scores, NEG)
        weights = jnp.exp(scores - jnp.max(scores, axis=0, keepdims=True))
        denom = jnp.sum(weights, axis=0, keepdims=True)
        attended = jnp.dot(
            flipped[base + 2 * VHD : base + 3 * VHD],
            weights.astype(jnp.bfloat16),
            preferred_element_type=jnp.float32,
        )
        attended = (attended / denom).astype(jnp.bfloat16)
        mixed[head * 128 : (head + 1) * 128, :] = jnp.dot(
            order, attended, preferred_element_type=jnp.float32
        ).astype(jnp.bfloat16)
    partial = lax.dot_general(
        mixed[...],
        rows_out[...].astype(jnp.bfloat16),
        (((0,), (0,)), ((), ())),
        preferred_element_type=jnp.float32,
    ).astype(jnp.bfloat16)
    out[...] = partial.reshape(out.shape)


def norm_kernel(parts, patches, gain, out):
    total = patches[lax.axis_index("tp") * 2 + lax.axis_index("h")].astype(jnp.float32)
    for peer in range(8):
        total += parts[peer].astype(jnp.float32)
    total = rms_scale(total, gain[...]).astype(jnp.bfloat16)
    for peer in range(8):
        out[peer] = total


def merge_kernel(rows, own, other, out, merged, weight):
    core, yh = lax.axis_index("core"), lax.axis_index("yh")
    for x in range(4):
        for rel in range(2):
            base = x * 4 + (yh ^ rel) * 2
            weight[pl.ds(pl.multiple_of((base + core) * 320, 16), 320), :] = own[x, rel]
            weight[pl.ds(pl.multiple_of((base + 1 - core) * 320, 16), 320), :] = other[x, rel]
    normed = rows[...].reshape(SLOT, VD).astype(jnp.float32)
    for c in range(VD // 128):
        merged[c] = normed[:, c * 128 : (c + 1) * 128]
    total = jnp.zeros((TOK, HD), jnp.float32)
    for r in range(MERGE):
        part = [merged[c, pl.ds(r, TOK, stride=MERGE), :] for c in range(VD // 128)]
        part = jnp.concatenate(part, axis=1).astype(jnp.bfloat16)
        total += jnp.dot(
            part, weight[r * VD : (r + 1) * VD, :], preferred_element_type=jnp.float32
        )
    total = total.astype(jnp.bfloat16)
    for peer in range(out.shape[0]):
        out[peer] = total


def prompt_index():
    return (lax.axis_index("x") * 2 + lax.axis_index("yh")) * 2 + lax.axis_index("core")


def query_positions():
    seq = lax.axis_index("j") * 2 + lax.axis_index("h")
    return seq * 128 + lax.broadcasted_iota(jnp.int32, (1, GROUP * 128), 1) % 128


def select_kernel(tokens, slots, images, after, out):
    del after
    prompt, plane = prompt_index(), lax.axis_index("j")
    shape = (IMG_TOTAL, images.shape[0] * TOK)
    row = lax.broadcasted_iota(jnp.int32, shape, 0)
    column = lax.broadcasted_iota(jnp.int32, shape, 1)
    wanted = jnp.full(shape, -1, jnp.int32)
    begin = jnp.int32(0)
    for k in range(IMG_ENC):
        slot = slots[prompt * IMG_ENC + k]
        count = tokens[prompt, k]
        base = jnp.where(slot % IMG_ENC == plane, (slot // IMG_ENC) * TOK - begin, -FAR)
        inside = (row >= begin) & (row < begin + count)
        wanted = jnp.where(inside, row + base, wanted)
        begin = begin + count
    selector = (column == wanted).astype(jnp.bfloat16)
    packed = jnp.dot(
        selector, images[...].reshape(shape[1], HD), preferred_element_type=jnp.float32
    ).astype(jnp.bfloat16)
    for peer in range(out.shape[0]):
        out[peer] = packed


def text_kernel(tokens, gaps, queries, cached, after, out, top_out, sum_out, flipped):
    del after
    prompt = prompt_index()
    for g in range(GROUP):
        block = queries[0, :, g * HD : (g + 1) * HD].astype(jnp.float32)
        flipped[:, g * 128 : (g + 1) * 128] = jnp.transpose(block).astype(jnp.bfloat16)
    factor = LOG2E / math.sqrt(HD)
    begin = jnp.int32(0)
    spans = []
    for k in range(IMG_ENC):
        begin = begin + gaps[prompt, k]
        spans.append((begin, begin + tokens[prompt, k]))
        begin = begin + tokens[prompt, k]
    top = jnp.full((1, GROUP * 128), NEG, jnp.float32)
    total = jnp.zeros((1, GROUP * 128), jnp.float32)
    out[...] = jnp.zeros(out.shape, jnp.float32)
    query = query_positions()
    for part in range(6):
        if part < 4:
            size = 768
            window = cached[2 * part : 2 * part + 2, 0:384, :].reshape(size, 2 * HD)
        else:
            size = 512
            window = cached[4 * part - 16 : 4 * part - 12, 384:512, :].reshape(size, 2 * HD)
        scores = jnp.dot(window[:, 0:HD], flipped[...], preferred_element_type=jnp.float32)
        if part >= 4:
            position = (part - 4) * size + lax.broadcasted_iota(jnp.int32, (size, 1), 0)
            for low, high in spans:
                position = jnp.where((position >= low) & (position < high), FAR, position)
            scores = jnp.where(position <= query, scores, NEG)
        highest = jnp.maximum(top, jnp.max(scores, axis=0, keepdims=True))
        scale = jnp.exp2((top - highest) * factor)
        weights = jnp.exp2((scores - highest) * factor)
        top = highest
        total = total * scale + jnp.sum(weights, axis=0, keepdims=True)
        out[...] = out[...] * scale + lax.dot_general(
            window[:, HD:],
            weights.astype(jnp.bfloat16),
            (((0,), (0,)), ((), ())),
            preferred_element_type=jnp.float32,
        )
    top_out[...] = top
    sum_out[...] = total


def join_kernel(tokens, gaps, images, flipped, accum, top, total, out):
    prompt = prompt_index()
    factor = LOG2E / math.sqrt(HD)
    keys = (images[0] + images[2]) + (images[4] + images[6])
    values = (images[1] + images[3]) + (images[5] + images[7])
    index = lax.broadcasted_iota(jnp.int32, (IMG_TOTAL, 1), 0)
    position = index
    begin = jnp.int32(0)
    for k in range(IMG_ENC):
        position = position + jnp.where(index >= begin, gaps[prompt, k], 0)
        begin = begin + tokens[prompt, k]
    scores = jnp.dot(keys, flipped[...], preferred_element_type=jnp.float32)
    scores = jnp.where(position <= query_positions(), scores, NEG)
    highest = jnp.maximum(top[...], jnp.max(scores, axis=0, keepdims=True))
    scale = jnp.exp2((top[...] - highest) * factor)
    weights = jnp.exp2((scores - highest) * factor)
    denom = total[...] * scale + jnp.sum(weights, axis=0, keepdims=True)
    joined = accum[...] * scale + lax.dot_general(
        values,
        weights.astype(jnp.bfloat16),
        (((0,), (0,)), ((), ())),
        preferred_element_type=jnp.float32,
    )
    joined = joined / denom
    for g in range(GROUP):
        block = jnp.transpose(joined[:, g * 128 : (g + 1) * 128])
        out[0, :, g * HD : (g + 1) * HD] = block.astype(jnp.bfloat16)


def per_device(
    patches,
    image_tokens,
    image_gap,
    image_slot,
    norm_gain,
    merge_gain,
    w_qkv,
    w_out,
    kv_merge,
    queries,
    text_kv,
    cache_kv,
):
    bf16, f32 = jnp.bfloat16, jnp.float32
    lanes = GROUP * 128

    def spread(value):
        both = jnp.stack([value, swap(value, "yh")])
        own = lax.all_to_all(jnp.broadcast_to(both[None], (4,) + both.shape), "x", 0, 0)
        return own, swap(own, "core")

    def call(kernel, name, out_shape, in_specs, scratch=(), cost=(0, 0, 0)):
        return pl.pallas_call(
            kernel,
            out_shape=out_shape,
            in_specs=in_specs,
            out_specs=jax.tree.map(lambda leaf: VMEM, out_shape),
            scratch_shapes=scratch,
            compiler_params=params(),
            cost_estimate=pl.CostEstimate(
                flops=cost[0], bytes_accessed=cost[1], transcendentals=cost[2]
            ),
            name=name,
        )

    def array(shape, dtype=bf16):
        return jax.ShapeDtypeStruct(shape, dtype)

    past = jnp.concatenate([cache_kv[0], text_kv[0]], axis=0)
    past = lax.all_gather(past, SEQ, axis=0)

    heads = call(
        pack_heads_kernel,
        "pack_heads",
        array((528, 128)),
        [VMEM] * 2,
        [pltpu.VMEM((208, 128), f32)],
        (1_000_000, 400_000, 0),
    )(w_qkv, w_out)
    own, other = spread(heads)

    sent = jnp.broadcast_to(patches[:, None], (4, 2, 32, VD)).reshape(8, 32, VD)
    image = lax.all_to_all(sent, SEQ, 0, 0)

    parts = call(
        vision_kernel,
        "vision",
        array((8, 32, VD)),
        [SMEM] * 2 + [VMEM] * 4,
        [
            pltpu.VMEM((VD, 512), bf16),
            pltpu.VMEM((208, 128), f32),
            pltpu.VMEM((256, VD), f32),
            pltpu.VMEM((256, SLOT), bf16),
        ],
        (600_000_000, 5_000_000, 131072),
    )(image_tokens, image_slot, image, norm_gain.reshape(1, VD), own, other)
    parts = lax.all_to_all(parts, ("tp", "h"), 0, 0)

    columns = call(
        pack_merge_kernel, "pack_merge", array((320, 128)), [VMEM, ANY], (), (0, 300_000, 0)
    )(kv_merge, other)
    merge_own, merge_other = spread(columns)

    rows = call(
        norm_kernel, "norm", array((8, 32, VD)), [VMEM] * 3, (), (1_000_000, 2_000_000, 32)
    )(parts, image, merge_gain.reshape(1, VD))
    rows = lax.all_to_all(rows, ("tp", "h"), 0, 0)

    image_kv = call(
        merge_kernel,
        "merge",
        array((16, TOK, HD)),
        [VMEM] * 3,
        [pltpu.VMEM((VD // 128, SLOT, 128), f32), pltpu.VMEM((MERGE * VD, HD), bf16)],
        (84_000_000, 3_000_000, 0),
    )(rows, merge_own, merge_other)
    every = lax.all_to_all(image_kv, ENC, 0, 0)

    accum, top, total, flipped = call(
        text_kernel,
        "text",
        (array((HD, lanes), f32), array((1, lanes), f32), array((1, lanes), f32), array((HD, lanes))),
        [SMEM] * 2 + [VMEM] * 2 + [ANY],
        (),
        (2_200_000_000, 4_000_000, lanes * 4096),
    )(image_tokens, image_gap, queries, past, image_kv)

    packed = call(
        select_kernel,
        "select",
        array((8, IMG_TOTAL, HD)),
        [SMEM] * 2 + [VMEM, ANY],
        (),
        (42_000_000, 600_000, 0),
    )(image_tokens, image_slot, every, total)
    images = lax.all_to_all(packed, SEQ, 0, 0)

    return call(
        join_kernel,
        "join",
        array((1, 128, lanes)),
        [SMEM] * 2 + [VMEM] * 5,
        (),
        (84_000_000, 2_000_000, lanes * 160),
    )(image_tokens, image_gap, images, flipped, accum, top, total)


def solution(mesh):
    fine = Mesh(
        mesh.devices.reshape(4, 2, 2, 4, 2, 4), ("x", "yh", "core", "j", "h", "tp")
    )
    in_specs = (
        P(ENC, SEQ, None),
        P(),
        P(),
        P(),
        P(),
        P(),
        P(ENC, "tp"),
        P(("tp",) + ENC, None),
        P(ENC, "tp"),
        P(ENC, SEQ, "tp"),
        P(ENC, SEQ, "tp"),
        P(ENC, SEQ, "tp"),
    )
    return jax.shard_map(
        per_device, mesh=fine, in_specs=in_specs, out_specs=P(ENC, SEQ, "tp"), check_vma=False
    )
```

```python
import math

import jax
import jax.numpy as jnp
from jax import lax
from jax.experimental import pallas as pl
from jax.experimental.pallas import tpu as pltpu
from jax.sharding import Mesh
from jax.sharding import PartitionSpec as P

VD = 1280
VHD = 80
MERGE = 4
HD = 128
GROUP = 8
IMG_ENC = 4
SLOT = 256
TOK = SLOT // MERGE
IMG_TOTAL = 160
SPAN = 1024
CACHE = 3072

EPS = 1e-06
FAR = 1 << 30
NEG = -1e30
LOG2E = math.log2(math.e)

ENC = ("x", "yh", "core")
SEQ = ("j", "h")
VMEM = pl.BlockSpec(memory_space=pltpu.VMEM)
SMEM = pl.BlockSpec(memory_space=pltpu.SMEM)
ANY = pl.BlockSpec(memory_space=pl.ANY)


def params(mib=48):
    return pltpu.CompilerParams(vmem_limit_bytes=mib << 20)


def swap(value, axis):
    return lax.ppermute(value, axis, [(0, 1), (1, 0)])


def rms_scale(values, gain):
    return values * lax.rsqrt(jnp.mean(values * values, axis=-1, keepdims=True) + EPS) * gain


def pack_kernel(w_qkv, w_out, kv_merge, out, lines):
    first = jnp.where(lax.axis_index("h") == 0, w_qkv[:, 0:480], w_qkv[:, 480:960])
    for c in range(4):
        size = min(128, 480 - c * 128)
        out[c * 80 : (c + 1) * 80, 0:size] = first[:, c * 128 : c * 128 + size]
    out[240:320, 96:128] = jnp.zeros((80, 32), jnp.bfloat16)
    lines[200:208, :] = jnp.zeros((8, 128), jnp.float32)
    rows = w_out[...].astype(jnp.float32)
    for c in range(10):
        lines[pl.ds(c, 20, stride=10), :] = rows[:, c * 128 : (c + 1) * 128]
    out[320:528, :] = lines[...].astype(jnp.bfloat16)
    out[528:848, :] = jnp.where(lax.axis_index("h") == 0, kv_merge[:, 0:HD], kv_merge[:, HD:])


def vision_kernel(tokens, slots, patches, gain, own, other, out, weight, lines, rows_out, mixed):
    core, yh, half = lax.axis_index("core"), lax.axis_index("yh"), lax.axis_index("h")
    here = lax.axis_index("x")
    slot = ((here * 2 + yh) * 2 + core) * IMG_ENC + lax.axis_index("j")
    for x in range(4):
        for rel in range(2):
            for c in range(4):
                base = (here ^ x) * 4 + (yh ^ rel) * 2
                tile = pl.ds(c * 128, 128)
                weight[pl.ds(pl.multiple_of((base + core) * 80, 16), 80), tile] = own[
                    x, rel, c * 80 : (c + 1) * 80, :
                ]
                weight[pl.ds(pl.multiple_of((base + 1 - core) * 80, 16), 80), tile] = other[
                    x, rel, c * 80 : (c + 1) * 80, :
                ]
    rows_out[...] = jnp.zeros(rows_out.shape, jnp.float32)
    for head in range(2):
        for rel in range(2):
            for part, piece in enumerate((own, other)):
                base = head * 128 + (rel * 2 + part) * 32
                lines[...] = piece[here ^ (half * 2 + head), rel, 320:528, :].astype(jnp.float32)
                for c in range(10):
                    rows_out[base : base + 20, c * 128 : (c + 1) * 128] = lines[
                        pl.ds(c, 20, stride=10), :
                    ]
    row = lax.broadcasted_iota(jnp.int32, (128, VHD), 0)
    column = lax.broadcasted_iota(jnp.int32, (128, VHD), 1)
    wanted = ((row // 32) ^ (yh * 2 + core)) * 20 + row % 32
    order = ((column == wanted) & (row % 32 < 20)).astype(jnp.bfloat16)
    count = jnp.int32(0)
    for i in range(slots.shape[0]):
        count = jnp.where(slots[i] == slot, tokens[i // IMG_ENC, i % IMG_ENC], count)
    rows = patches[...].reshape(SLOT, VD).astype(jnp.float32)
    normed = rms_scale(rows, gain[...]).astype(jnp.bfloat16)
    qkv = jnp.dot(normed, weight[...], preferred_element_type=jnp.float32)
    flipped = jnp.transpose(qkv).astype(jnp.bfloat16)
    live = lax.broadcasted_iota(jnp.int32, (SLOT, SLOT), 0) < MERGE * count
    for head in range(2):
        base = head * 3 * VHD
        keys = qkv[:, base + VHD : base + 2 * VHD].astype(jnp.bfloat16)
        scores = jnp.dot(
            keys, flipped[base : base + VHD], preferred_element_type=jnp.float32
        ) * (1.0 / math.sqrt(VHD))
        scores = jnp.where(live, scores, NEG)
        weights = jnp.exp(scores - jnp.max(scores, axis=0, keepdims=True))
        denom = jnp.sum(weights, axis=0, keepdims=True)
        attended = jnp.dot(
            flipped[base + 2 * VHD : base + 3 * VHD],
            weights.astype(jnp.bfloat16),
            preferred_element_type=jnp.float32,
        )
        attended = (attended / denom).astype(jnp.bfloat16)
        mixed[head * 128 : (head + 1) * 128, :] = jnp.dot(
            order, attended, preferred_element_type=jnp.float32
        ).astype(jnp.bfloat16)
    partial = lax.dot_general(
        mixed[...],
        rows_out[...].astype(jnp.bfloat16),
        (((0,), (0,)), ((), ())),
        preferred_element_type=jnp.float32,
    ).astype(jnp.bfloat16)
    out[...] = partial.reshape(out.shape)


def norm_kernel(parts, patches, gain, weights, out):
    del weights
    total = patches[lax.axis_index("tp") * 2 + lax.axis_index("h")].astype(jnp.float32)
    for peer in range(8):
        total += parts[peer].astype(jnp.float32)
    total = rms_scale(total, gain[...]).astype(jnp.bfloat16)
    for peer in range(8):
        out[peer] = total


def merge_kernel(rows, own, other, out, merged, weight):
    core, yh = lax.axis_index("core"), lax.axis_index("yh")
    for k in range(4):
        for rel in range(2):
            base = (lax.axis_index("x") ^ k) * 4 + (yh ^ rel) * 2
            weight[pl.ds(pl.multiple_of((base + core) * 320, 16), 320), :] = own[k, rel]
            weight[pl.ds(pl.multiple_of((base + 1 - core) * 320, 16), 320), :] = other[k, rel]
    normed = rows[...].reshape(SLOT, VD).astype(jnp.float32)
    for c in range(VD // 128):
        merged[c] = normed[:, c * 128 : (c + 1) * 128]
    total = jnp.zeros((TOK, HD), jnp.float32)
    for r in range(MERGE):
        part = [merged[c, pl.ds(r, TOK, stride=MERGE), :] for c in range(VD // 128)]
        part = jnp.concatenate(part, axis=1).astype(jnp.bfloat16)
        total += jnp.dot(
            part, weight[r * VD : (r + 1) * VD, :], preferred_element_type=jnp.float32
        )
    total = total.astype(jnp.bfloat16)
    for peer in range(out.shape[0]):
        out[peer] = total


def prompt_index():
    return (lax.axis_index("x") * 2 + lax.axis_index("yh")) * 2 + lax.axis_index("core")


def query_positions():
    seq = lax.axis_index("j") * 2 + lax.axis_index("h")
    return seq * 128 + lax.broadcasted_iota(jnp.int32, (1, GROUP * 128), 1) % 128


def select_kernel(tokens, slots, images, after, out):
    del after
    prompt, plane = prompt_index(), lax.axis_index("j")
    shape = (IMG_TOTAL, images.shape[0] * TOK)
    row = lax.broadcasted_iota(jnp.int32, shape, 0)
    column = lax.broadcasted_iota(jnp.int32, shape, 1)
    wanted = jnp.full(shape, -1, jnp.int32)
    begin = jnp.int32(0)
    for k in range(IMG_ENC):
        slot = slots[prompt * IMG_ENC + k]
        count = tokens[prompt, k]
        base = jnp.where(slot % IMG_ENC == plane, (slot // IMG_ENC) * TOK - begin, -FAR)
        inside = (row >= begin) & (row < begin + count)
        wanted = jnp.where(inside, row + base, wanted)
        begin = begin + count
    selector = (column == wanted).astype(jnp.bfloat16)
    packed = jnp.dot(
        selector, images[...].reshape(shape[1], HD), preferred_element_type=jnp.float32
    ).astype(jnp.bfloat16)
    for peer in range(out.shape[0]):
        out[peer] = packed


def text_kernel(tokens, gaps, queries, cached, after, out, top_out, sum_out, flipped):
    del after
    prompt = prompt_index()
    for g in range(GROUP):
        block = queries[0, :, g * HD : (g + 1) * HD].astype(jnp.float32)
        flipped[:, g * 128 : (g + 1) * 128] = jnp.transpose(block).astype(jnp.bfloat16)
    factor = LOG2E / math.sqrt(HD)
    begin = jnp.int32(0)
    spans = []
    for k in range(IMG_ENC):
        begin = begin + gaps[prompt, k]
        spans.append((begin, begin + tokens[prompt, k]))
        begin = begin + tokens[prompt, k]
    top = jnp.full((1, GROUP * 128), NEG, jnp.float32)
    total = jnp.zeros((1, GROUP * 128), jnp.float32)
    out[...] = jnp.zeros(out.shape, jnp.float32)
    query = query_positions()
    for part in range(6):
        if part < 4:
            size = 768
            window = cached[2 * part : 2 * part + 2, 0:384, :].reshape(size, 2 * HD)
        else:
            size = 512
            window = cached[4 * part - 16 : 4 * part - 12, 384:512, :].reshape(size, 2 * HD)
        scores = jnp.dot(window[:, 0:HD], flipped[...], preferred_element_type=jnp.float32)
        if part >= 4:
            position = (part - 4) * size + lax.broadcasted_iota(jnp.int32, (size, 1), 0)
            for low, high in spans:
                position = jnp.where((position >= low) & (position < high), FAR, position)
            scores = jnp.where(position <= query, scores, NEG)
        highest = jnp.maximum(top, jnp.max(scores, axis=0, keepdims=True))
        scale = jnp.exp2((top - highest) * factor)
        weights = jnp.exp2((scores - highest) * factor)
        top = highest
        total = total * scale + jnp.sum(weights, axis=0, keepdims=True)
        out[...] = out[...] * scale + lax.dot_general(
            window[:, HD:],
            weights.astype(jnp.bfloat16),
            (((0,), (0,)), ((), ())),
            preferred_element_type=jnp.float32,
        )
    top_out[...] = top
    sum_out[...] = total


def join_kernel(tokens, gaps, images, flipped, accum, top, total, out):
    prompt = prompt_index()
    factor = LOG2E / math.sqrt(HD)
    keys = (images[0] + images[2]) + (images[4] + images[6])
    values = (images[1] + images[3]) + (images[5] + images[7])
    index = lax.broadcasted_iota(jnp.int32, (IMG_TOTAL, 1), 0)
    position = index
    begin = jnp.int32(0)
    for k in range(IMG_ENC):
        position = position + jnp.where(index >= begin, gaps[prompt, k], 0)
        begin = begin + tokens[prompt, k]
    scores = jnp.dot(keys, flipped[...], preferred_element_type=jnp.float32)
    scores = jnp.where(position <= query_positions(), scores, NEG)
    highest = jnp.maximum(top[...], jnp.max(scores, axis=0, keepdims=True))
    scale = jnp.exp2((top[...] - highest) * factor)
    weights = jnp.exp2((scores - highest) * factor)
    denom = total[...] * scale + jnp.sum(weights, axis=0, keepdims=True)
    joined = accum[...] * scale + lax.dot_general(
        values,
        weights.astype(jnp.bfloat16),
        (((0,), (0,)), ((), ())),
        preferred_element_type=jnp.float32,
    )
    joined = joined / denom
    for g in range(GROUP):
        block = jnp.transpose(joined[:, g * 128 : (g + 1) * 128])
        out[0, :, g * HD : (g + 1) * HD] = block.astype(jnp.bfloat16)


def per_device(
    patches,
    image_tokens,
    image_gap,
    image_slot,
    norm_gain,
    merge_gain,
    w_qkv,
    w_out,
    kv_merge,
    queries,
    text_kv,
    cache_kv,
):
    bf16, f32 = jnp.bfloat16, jnp.float32
    lanes = GROUP * 128

    def after(value, event):
        return lax.optimization_barrier((value, event))[0]

    def swap_x(value, bits):
        return lax.ppermute(value, "x", [(i, i ^ bits) for i in range(4)])

    def call(kernel, name, out_shape, in_specs, scratch=(), cost=(0, 0, 0)):
        return pl.pallas_call(
            kernel,
            out_shape=out_shape,
            in_specs=in_specs,
            out_specs=jax.tree.map(lambda leaf: VMEM, out_shape),
            scratch_shapes=scratch,
            compiler_params=params(),
            cost_estimate=pl.CostEstimate(
                flops=cost[0], bytes_accessed=cost[1], transcendentals=cost[2]
            ),
            name=name,
        )

    def array(shape, dtype=bf16):
        return jax.ShapeDtypeStruct(shape, dtype)

    past = jnp.concatenate([cache_kv[0], text_kv[0]], axis=0)
    past = lax.all_gather(past, SEQ, axis=0)

    heads = call(
        pack_kernel,
        "pack",
        array((848, 128)),
        [VMEM] * 3,
        [pltpu.VMEM((208, 128), f32)],
        (1_000_000, 800_000, 0),
    )(w_qkv, w_out, kv_merge)
    mine, theirs = heads, swap(heads, "yh")

    sent = jnp.broadcast_to(patches[:, None], (4, 2, 32, VD)).reshape(8, 32, VD)
    image = lax.all_to_all(sent, SEQ, 0, 0)
    first = [mine[0:528]] + [swap_x(mine[0:528], k) for k in (1, 2, 3)]
    second = [theirs[0:528]] + [swap_x(theirs[0:528], k) for k in (1, 2, 3)]
    own = jnp.stack([jnp.stack(first), jnp.stack(second)], axis=1)
    merge_pair = jnp.stack([mine[528:848], theirs[528:848]])
    merge_pair = jnp.stack([merge_pair, swap_x(merge_pair, 1)])
    other = swap(after(own, (image, merge_pair)), "core")

    parts = call(
        vision_kernel,
        "vision",
        array((8, 32, VD)),
        [SMEM] * 2 + [VMEM] * 4,
        [
            pltpu.VMEM((VD, 512), bf16),
            pltpu.VMEM((208, 128), f32),
            pltpu.VMEM((256, VD), f32),
            pltpu.VMEM((256, SLOT), bf16),
        ],
        (600_000_000, 5_000_000, 131072),
    )(image_tokens, image_slot, image, norm_gain.reshape(1, VD), own, other)
    merge_own = jnp.concatenate([merge_pair, swap_x(after(merge_pair, parts), 2)])
    parts = lax.all_to_all(parts, ("tp", "h"), 0, 0)

    rows = call(
        norm_kernel, "norm", array((8, 32, VD)), [VMEM] * 3 + [ANY], (), (1_000_000, 2_000_000, 32)
    )(parts, image, merge_gain.reshape(1, VD), merge_own)
    merge_other = swap(after(merge_own, rows), "core")
    rows = lax.all_to_all(rows, ("tp", "h"), 0, 0)

    image_kv = call(
        merge_kernel,
        "merge",
        array((16, TOK, HD)),
        [VMEM] * 3,
        [pltpu.VMEM((VD // 128, SLOT, 128), f32), pltpu.VMEM((MERGE * VD, HD), bf16)],
        (84_000_000, 3_000_000, 0),
    )(rows, merge_own, merge_other)
    every = lax.all_to_all(image_kv, ENC, 0, 0)

    accum, top, total, flipped = call(
        text_kernel,
        "text",
        (array((HD, lanes), f32), array((1, lanes), f32), array((1, lanes), f32), array((HD, lanes))),
        [SMEM] * 2 + [VMEM] * 2 + [ANY],
        (),
        (2_200_000_000, 4_000_000, lanes * 4096),
    )(image_tokens, image_gap, queries, past, image_kv)

    packed = call(
        select_kernel,
        "select",
        array((8, IMG_TOTAL, HD)),
        [SMEM] * 2 + [VMEM, ANY],
        (),
        (42_000_000, 600_000, 0),
    )(image_tokens, image_slot, every, total)
    images = lax.all_to_all(packed, SEQ, 0, 0)

    return call(
        join_kernel,
        "join",
        array((1, 128, lanes)),
        [SMEM] * 2 + [VMEM] * 5,
        (),
        (84_000_000, 2_000_000, lanes * 160),
    )(image_tokens, image_gap, images, flipped, accum, top, total)


def solution(mesh):
    fine = Mesh(
        mesh.devices.reshape(4, 2, 2, 4, 2, 4), ("x", "yh", "core", "j", "h", "tp")
    )
    in_specs = (
        P(ENC, SEQ, None),
        P(),
        P(),
        P(),
        P(),
        P(),
        P(ENC, "tp"),
        P(("tp",) + ENC, None),
        P(ENC, "tp"),
        P(ENC, SEQ, "tp"),
        P(ENC, SEQ, "tp"),
        P(ENC, SEQ, "tp"),
    )
    return jax.shard_map(
        per_device, mesh=fine, in_specs=in_specs, out_specs=P(ENC, SEQ, "tp"), check_vma=False
    )
```

```python
import functools
import math

import jax
import jax.numpy as jnp
from jax import lax
from jax.experimental import pallas as pl
from jax.experimental.pallas import tpu as pltpu
from jax.sharding import Mesh
from jax.sharding import PartitionSpec as P

VD = 1280
VHD = 80
MERGE = 4
HD = 128
GROUP = 8
IMG_ENC = 4
SLOT = 256
TOK = SLOT // MERGE
IMG_TOTAL = 160
SPAN = 1024
CACHE = 3072

EPS = 1e-06
FAR = 1 << 30
NEG = -1e30
LOG2E = math.log2(math.e)

ENC = ("x", "yh", "core")
ENC_BACK = ("core", "yh", "x")
SEQ = ("j", "h")
SEQ_BACK = ("h", "j")
VMEM = pl.BlockSpec(memory_space=pltpu.VMEM)
SMEM = pl.BlockSpec(memory_space=pltpu.SMEM)
ANY = pl.BlockSpec(memory_space=pl.ANY)


def params(mib=48):
    return pltpu.CompilerParams(vmem_limit_bytes=mib << 20)


def swap(value, axis):
    return lax.ppermute(value, axis, [(0, 1), (1, 0)])


def rms_scale(values, gain):
    return values * lax.rsqrt(jnp.mean(values * values, axis=-1, keepdims=True) + EPS) * gain


def pack_kernel(
    w_qkv_hbm, w_out_hbm, kv_merge_hbm, patches_hbm, out, sent,
    w_qkv, w_out, kv_merge, patches, lines, arrived,
):
    moves = [
        (w_qkv_hbm, w_qkv), (w_out_hbm, w_out), (kv_merge_hbm, kv_merge), (patches_hbm, patches)
    ]
    copies = [
        pltpu.make_async_copy(source, target, arrived.at[i])
        for i, (source, target) in enumerate(moves)
    ]
    for copy in copies:
        copy.start()
    for copy in copies:
        copy.wait()
    first = jnp.where(lax.axis_index("h") == 0, w_qkv[:, 0:480], w_qkv[:, 480:960])
    for c in range(4):
        size = min(128, 480 - c * 128)
        out[c * 80 : (c + 1) * 80, 0:size] = first[:, c * 128 : c * 128 + size]
    out[240:320, 96:128] = jnp.zeros((80, 32), jnp.bfloat16)
    lines[200:208, :] = jnp.zeros((8, 128), jnp.float32)
    rows = w_out[...].astype(jnp.float32)
    for c in range(10):
        lines[pl.ds(c, 20, stride=10), :] = rows[:, c * 128 : (c + 1) * 128]
    out[320:528, :] = lines[...].astype(jnp.bfloat16)
    out[528:848, :] = jnp.where(lax.axis_index("h") == 0, kv_merge[:, 0:HD], kv_merge[:, HD:])
    for rank in range(8):
        sent[rank] = patches[rank % 4]


def vision_kernel(tokens, slots, patches, gain, own, other, out, weight, lines, rows_out, mixed):
    core, yh, half = lax.axis_index("core"), lax.axis_index("yh"), lax.axis_index("h")
    slot = ((lax.axis_index("x") * 2 + yh) * 2 + core) * IMG_ENC + lax.axis_index("j")
    for x in range(4):
        for rel in range(2):
            for c in range(4):
                base = x * 4 + (yh ^ rel) * 2
                tile = pl.ds(c * 128, 128)
                weight[pl.ds(pl.multiple_of((base + core) * 80, 16), 80), tile] = own[
                    rel, x, c * 80 : (c + 1) * 80, :
                ]
                weight[pl.ds(pl.multiple_of((base + 1 - core) * 80, 16), 80), tile] = other[
                    rel, x, c * 80 : (c + 1) * 80, :
                ]
    rows_out[...] = jnp.zeros(rows_out.shape, jnp.float32)
    for head in range(2):
        for rel in range(2):
            for part, piece in enumerate((own, other)):
                base = head * 128 + (rel * 2 + part) * 32
                lines[...] = piece[rel, half * 2 + head, 320:528, :].astype(jnp.float32)
                for c in range(10):
                    rows_out[base : base + 20, c * 128 : (c + 1) * 128] = lines[
                        pl.ds(c, 20, stride=10), :
                    ]
    row = lax.broadcasted_iota(jnp.int32, (128, VHD), 0)
    column = lax.broadcasted_iota(jnp.int32, (128, VHD), 1)
    wanted = ((row // 32) ^ (yh * 2 + core)) * 20 + row % 32
    order = ((column == wanted) & (row % 32 < 20)).astype(jnp.bfloat16)
    count = jnp.int32(0)
    for i in range(slots.shape[0]):
        count = jnp.where(slots[i] == slot, tokens[i // IMG_ENC, i % IMG_ENC], count)
    rows = [patches[z % 2 * 4 + z // 2].astype(jnp.float32) for z in range(8)]
    normed = rms_scale(jnp.concatenate(rows), gain[...]).astype(jnp.bfloat16)
    qkv = jnp.dot(normed, weight[...], preferred_element_type=jnp.float32)
    flipped = jnp.transpose(qkv).astype(jnp.bfloat16)
    live = lax.broadcasted_iota(jnp.int32, (SLOT, SLOT), 0) < MERGE * count
    for head in range(2):
        base = head * 3 * VHD
        keys = qkv[:, base + VHD : base + 2 * VHD].astype(jnp.bfloat16)
        scores = jnp.dot(
            keys, flipped[base : base + VHD], preferred_element_type=jnp.float32
        ) * (1.0 / math.sqrt(VHD))
        scores = jnp.where(live, scores, NEG)
        weights = jnp.exp(scores - jnp.max(scores, axis=0, keepdims=True))
        denom = jnp.sum(weights, axis=0, keepdims=True)
        attended = jnp.dot(
            flipped[base + 2 * VHD : base + 3 * VHD],
            weights.astype(jnp.bfloat16),
            preferred_element_type=jnp.float32,
        )
        attended = (attended / denom).astype(jnp.bfloat16)
        mixed[head * 128 : (head + 1) * 128, :] = jnp.dot(
            order, attended, preferred_element_type=jnp.float32
        ).astype(jnp.bfloat16)
    partial = lax.dot_general(
        mixed[...],
        rows_out[...].astype(jnp.bfloat16),
        (((0,), (0,)), ((), ())),
        preferred_element_type=jnp.float32,
    ).astype(jnp.bfloat16)
    out[...] = partial.reshape(out.shape)


def norm_kernel(parts, patches, gain, weights, out):
    del weights
    t = lax.axis_index("tp")
    total = patches[t % 2 * 4 + lax.axis_index("h") * 2 + t // 2].astype(jnp.float32)
    for peer in range(8):
        total += parts[peer].astype(jnp.float32)
    total = rms_scale(total, gain[...]).astype(jnp.bfloat16)
    for peer in range(8):
        out[peer] = total


def merge_kernel(rows, own, other, out, merged, weight):
    core, yh = lax.axis_index("core"), lax.axis_index("yh")
    for x in range(4):
        for rel in range(2):
            base = x * 4 + (yh ^ rel) * 2
            weight[pl.ds(pl.multiple_of((base + core) * 320, 16), 320), :] = own[rel, x]
            weight[pl.ds(pl.multiple_of((base + 1 - core) * 320, 16), 320), :] = other[rel, x]
    normed = rows[...].reshape(SLOT, VD).astype(jnp.float32)
    for c in range(VD // 128):
        merged[c] = normed[:, c * 128 : (c + 1) * 128]
    total = jnp.zeros((TOK, HD), jnp.float32)
    for r in range(MERGE):
        part = [merged[c, pl.ds(r, TOK, stride=MERGE), :] for c in range(VD // 128)]
        part = jnp.concatenate(part, axis=1).astype(jnp.bfloat16)
        total += jnp.dot(
            part, weight[r * VD : (r + 1) * VD, :], preferred_element_type=jnp.float32
        )
    total = total.astype(jnp.bfloat16)
    for peer in range(out.shape[0]):
        out[peer] = total


def prompt_index():
    return (lax.axis_index("x") * 2 + lax.axis_index("yh")) * 2 + lax.axis_index("core")


def query_positions():
    seq = lax.axis_index("j") * 2 + lax.axis_index("h")
    return seq * 128 + lax.broadcasted_iota(jnp.int32, (1, GROUP * 128), 1) % 128


def select_kernel(tokens, slots, images, after, out):
    del after
    prompt, plane = prompt_index(), lax.axis_index("j")
    shape = (IMG_TOTAL, images.shape[0] * TOK)
    row = lax.broadcasted_iota(jnp.int32, shape, 0)
    column = lax.broadcasted_iota(jnp.int32, shape, 1)
    wanted = jnp.full(shape, -1, jnp.int32)
    begin = jnp.int32(0)
    for k in range(IMG_ENC):
        slot = slots[prompt * IMG_ENC + k]
        count = tokens[prompt, k]
        enc = slot // IMG_ENC
        place = (enc % 2) * 8 + (enc // 2 % 2) * 4 + enc // 4
        base = jnp.where(slot % IMG_ENC == plane, place * TOK - begin, -FAR)
        inside = (row >= begin) & (row < begin + count)
        wanted = jnp.where(inside, row + base, wanted)
        begin = begin + count
    selector = (column == wanted).astype(jnp.bfloat16)
    packed = jnp.dot(
        selector, images[...].reshape(shape[1], HD), preferred_element_type=jnp.float32
    ).astype(jnp.bfloat16)
    for peer in range(out.shape[0]):
        out[peer] = packed


def text_kernel(blocks, tokens, gaps, queries, cached, *refs):
    if blocks[0] == 0:
        after, out, top_out, sum_out, flipped = refs
    else:
        accum, top_in, sum_in, queries_in, after, out, top_out, sum_out = refs
    del after
    prompt = prompt_index()
    if blocks[0] == 0:
        for g in range(GROUP):
            block = queries[0, :, g * HD : (g + 1) * HD].astype(jnp.float32)
            flipped[:, g * 128 : (g + 1) * 128] = jnp.transpose(block).astype(jnp.bfloat16)
    else:
        flipped = queries_in
    factor = LOG2E / math.sqrt(HD)
    begin = jnp.int32(0)
    spans = []
    for k in range(IMG_ENC):
        begin = begin + gaps[prompt, k]
        spans.append((begin, begin + tokens[prompt, k]))
        begin = begin + tokens[prompt, k]
    if blocks[0] == 0:
        top = jnp.full((1, GROUP * 128), NEG, jnp.float32)
        total = jnp.zeros((1, GROUP * 128), jnp.float32)
        out[...] = jnp.zeros(out.shape, jnp.float32)
    else:
        top, total = top_in[...], sum_in[...]
        out[...] = accum[...]
    query = query_positions()
    for part in blocks:
        if part < 4:
            size = 768
            window = cached[2 * part : 2 * part + 2, 0:384, :].reshape(size, 2 * HD)
        else:
            size = 512
            window = cached[4 * part - 16 : 4 * part - 12, 384:512, :].reshape(size, 2 * HD)
        scores = jnp.dot(window[:, 0:HD], flipped[...], preferred_element_type=jnp.float32)
        if part >= 4:
            position = (part - 4) * size + lax.broadcasted_iota(jnp.int32, (size, 1), 0)
            for low, high in spans:
                position = jnp.where((position >= low) & (position < high), FAR, position)
            scores = jnp.where(position <= query, scores, NEG)
        highest = jnp.maximum(top, jnp.max(scores, axis=0, keepdims=True))
        scale = jnp.exp2((top - highest) * factor)
        weights = jnp.exp2((scores - highest) * factor)
        top = highest
        total = total * scale + jnp.sum(weights, axis=0, keepdims=True)
        out[...] = out[...] * scale + lax.dot_general(
            window[:, HD:],
            weights.astype(jnp.bfloat16),
            (((0,), (0,)), ((), ())),
            preferred_element_type=jnp.float32,
        )
    top_out[...] = top
    sum_out[...] = total


def join_kernel(tokens, gaps, images, flipped, accum, top, total, out):
    prompt = prompt_index()
    factor = LOG2E / math.sqrt(HD)
    keys = (images[0] + images[1]) + (images[2] + images[3])
    values = (images[4] + images[5]) + (images[6] + images[7])
    index = lax.broadcasted_iota(jnp.int32, (IMG_TOTAL, 1), 0)
    position = index
    begin = jnp.int32(0)
    for k in range(IMG_ENC):
        position = position + jnp.where(index >= begin, gaps[prompt, k], 0)
        begin = begin + tokens[prompt, k]
    scores = jnp.dot(keys, flipped[...], preferred_element_type=jnp.float32)
    scores = jnp.where(position <= query_positions(), scores, NEG)
    highest = jnp.maximum(top[...], jnp.max(scores, axis=0, keepdims=True))
    scale = jnp.exp2((top[...] - highest) * factor)
    weights = jnp.exp2((scores - highest) * factor)
    denom = total[...] * scale + jnp.sum(weights, axis=0, keepdims=True)
    joined = accum[...] * scale + lax.dot_general(
        values,
        weights.astype(jnp.bfloat16),
        (((0,), (0,)), ((), ())),
        preferred_element_type=jnp.float32,
    )
    joined = joined / denom
    for g in range(GROUP):
        block = jnp.transpose(joined[:, g * 128 : (g + 1) * 128])
        out[0, :, g * HD : (g + 1) * HD] = block.astype(jnp.bfloat16)


def per_device(
    patches,
    image_tokens,
    image_gap,
    image_slot,
    norm_gain,
    merge_gain,
    w_qkv,
    w_out,
    kv_merge,
    queries,
    text_kv,
    cache_kv,
):
    bf16, f32 = jnp.bfloat16, jnp.float32
    lanes = GROUP * 128

    def after(value, event):
        return lax.optimization_barrier((value, event))[0]

    def swap_x(value, bits):
        return lax.ppermute(value, "x", [(i, i ^ bits) for i in range(4)])

    def call(kernel, name, out_shape, in_specs, scratch=(), cost=(0, 0, 0)):
        return pl.pallas_call(
            kernel,
            out_shape=out_shape,
            in_specs=in_specs,
            out_specs=jax.tree.map(lambda leaf: VMEM, out_shape),
            scratch_shapes=scratch,
            compiler_params=params(),
            cost_estimate=pl.CostEstimate(
                flops=cost[0], bytes_accessed=cost[1], transcendentals=cost[2]
            ),
            name=name,
        )

    def array(shape, dtype=bf16):
        return jax.ShapeDtypeStruct(shape, dtype)

    past = jnp.concatenate([cache_kv[0], text_kv[0]], axis=0)
    past = lax.all_gather(past, SEQ, axis=0)

    heads, sent = pl.pallas_call(
        pack_kernel,
        out_shape=(array((848, 128)), array((8, 32, VD))),
        in_specs=[ANY] * 4,
        out_specs=(VMEM, VMEM),
        scratch_shapes=[
            pltpu.VMEM((80, 960), bf16),
            pltpu.VMEM((20, VD), bf16),
            pltpu.VMEM((320, 256), bf16),
            pltpu.VMEM((4, 32, VD), bf16),
            pltpu.VMEM((208, 128), f32),
            pltpu.SemaphoreType.DMA((4,)),
        ],
        cost_estimate=pl.CostEstimate(flops=1_000_000, bytes_accessed=2_000_000, transcendentals=0),
        name="pack",
    )(w_qkv, w_out, kv_merge, patches)
    mine, theirs = heads, swap(heads, "yh")

    image = lax.all_to_all(sent, SEQ_BACK, 0, 0)
    first = lax.all_gather(mine, "x", axis=0)
    second = lax.all_gather(theirs, "x", axis=0)
    own = jnp.stack([first[:, 0:528], second[:, 0:528]])
    other = swap(after(own, image), "core")

    parts = call(
        vision_kernel,
        "vision",
        array((8, 32, VD)),
        [SMEM] * 2 + [VMEM] * 4,
        [
            pltpu.VMEM((VD, 512), bf16),
            pltpu.VMEM((208, 128), f32),
            pltpu.VMEM((256, VD), f32),
            pltpu.VMEM((256, SLOT), bf16),
        ],
        (600_000_000, 5_000_000, 131072),
    )(image_tokens, image_slot, image, norm_gain.reshape(1, VD), own, other)
    first, second = after((first, second), parts)
    merge_own = jnp.stack([first[:, 528:848], second[:, 528:848]])
    parts = lax.all_to_all(parts, ("h", "tp"), 0, 0)

    rows = call(
        norm_kernel, "norm", array((8, 32, VD)), [VMEM] * 3 + [ANY], (), (1_000_000, 2_000_000, 32)
    )(parts, image, merge_gain.reshape(1, VD), merge_own)
    merge_other = swap(after(merge_own, rows), "core")
    rows = lax.all_to_all(rows, ("h", "tp"), 0, 0)

    image_kv = call(
        merge_kernel,
        "merge",
        array((16, TOK, HD)),
        [VMEM] * 3,
        [pltpu.VMEM((VD // 128, SLOT, 128), f32), pltpu.VMEM((MERGE * VD, HD), bf16)],
        (84_000_000, 3_000_000, 0),
    )(rows, merge_own, merge_other)
    every = lax.all_to_all(image_kv, ENC_BACK, 0, 0)

    state = (array((HD, lanes), f32), array((1, lanes), f32), array((1, lanes), f32))
    *state_a, flipped = call(
        functools.partial(text_kernel, (0, 1, 2)),
        "cached",
        state + (array((HD, lanes)),),
        [SMEM] * 2 + [VMEM] * 2 + [ANY],
        (),
        (1_200_000_000, 3_000_000, lanes * 2304),
    )(image_tokens, image_gap, queries, past, image_kv)
    packed = call(
        select_kernel,
        "select",
        array((8, IMG_TOTAL, HD)),
        [SMEM] * 2 + [VMEM, ANY],
        (),
        (42_000_000, 600_000, 0),
    )(image_tokens, image_slot, every, flipped)
    accum, top, total = call(
        functools.partial(text_kernel, (3, 4, 5)),
        "text",
        state,
        [SMEM] * 2 + [VMEM] * 6 + [ANY],
        (),
        (1_000_000_000, 3_000_000, lanes * 1792),
    )(image_tokens, image_gap, queries, past, *state_a, flipped, packed)
    images = lax.all_to_all(packed, SEQ_BACK, 0, 0)

    return call(
        join_kernel,
        "join",
        array((1, 128, lanes)),
        [SMEM] * 2 + [VMEM] * 5,
        (),
        (84_000_000, 2_000_000, lanes * 160),
    )(image_tokens, image_gap, images, flipped, accum, top, total)


def solution(mesh):
    fine = Mesh(
        mesh.devices.reshape(4, 2, 2, 4, 2, 4), ("x", "yh", "core", "j", "h", "tp")
    )
    in_specs = (
        P(ENC, SEQ, None),
        P(),
        P(),
        P(),
        P(),
        P(),
        P(ENC, "tp"),
        P(("tp",) + ENC, None),
        P(ENC, "tp"),
        P(ENC, SEQ, "tp"),
        P(ENC, SEQ, "tp"),
        P(ENC, SEQ, "tp"),
    )
    return jax.shard_map(
        per_device, mesh=fine, in_specs=in_specs, out_specs=P(ENC, SEQ, "tp"), check_vma=False
    )
```

```python
import functools
import math

import jax
import jax.numpy as jnp
from jax import lax
from jax.experimental import pallas as pl
from jax.experimental.pallas import tpu as pltpu
from jax.sharding import Mesh
from jax.sharding import PartitionSpec as P

VD = 1280
VHD = 80
MERGE = 4
HD = 128
GROUP = 8
IMG_ENC = 4
SLOT = 256
TOK = SLOT // MERGE
IMG_TOTAL = 160
SPAN = 1024
CACHE = 3072

EPS = 1e-06
FAR = 1 << 30
NEG = -1e30
LOG2E = math.log2(math.e)

ENC = ("x", "yh", "core")
ENC_BACK = ("core", "yh", "x")
SEQ = ("j", "h")
SEQ_BACK = ("h", "j")
VMEM = pl.BlockSpec(memory_space=pltpu.VMEM)
SMEM = pl.BlockSpec(memory_space=pltpu.SMEM)
ANY = pl.BlockSpec(memory_space=pl.ANY)


def params(mib=48):
    return pltpu.CompilerParams(vmem_limit_bytes=mib << 20)


def swap(value, axis):
    return lax.ppermute(value, axis, [(0, 1), (1, 0)])


def rms_scale(values, gain):
    return values * lax.rsqrt(jnp.mean(values * values, axis=-1, keepdims=True) + EPS) * gain


def pack_kernel(
    w_qkv_hbm, w_out_hbm, kv_merge_hbm, patches_hbm, out, sent,
    w_qkv, w_out, kv_merge, patches, lines, arrived,
):
    moves = [
        (w_qkv_hbm, w_qkv), (w_out_hbm, w_out), (kv_merge_hbm, kv_merge), (patches_hbm, patches)
    ]
    copies = [
        pltpu.make_async_copy(source, target, arrived.at[i])
        for i, (source, target) in enumerate(moves)
    ]
    for copy in copies:
        copy.start()
    for copy in copies:
        copy.wait()
    first = jnp.where(lax.axis_index("h") == 0, w_qkv[:, 0:480], w_qkv[:, 480:960])
    for c in range(4):
        size = min(128, 480 - c * 128)
        out[c * 80 : (c + 1) * 80, 0:size] = first[:, c * 128 : c * 128 + size]
    out[240:320, 96:128] = jnp.zeros((80, 32), jnp.bfloat16)
    lines[200:208, :] = jnp.zeros((8, 128), jnp.float32)
    rows = w_out[...].astype(jnp.float32)
    for c in range(10):
        lines[pl.ds(c, 20, stride=10), :] = rows[:, c * 128 : (c + 1) * 128]
    out[320:528, :] = lines[...].astype(jnp.bfloat16)
    out[528:848, :] = jnp.where(lax.axis_index("h") == 0, kv_merge[:, 0:HD], kv_merge[:, HD:])
    for rank in range(8):
        sent[rank] = patches[rank % 4]


def vision_kernel(tokens, slots, patches, gain, own, other, out, weight, lines, rows_out, mixed):
    core, yh, half = lax.axis_index("core"), lax.axis_index("yh"), lax.axis_index("h")
    slot = ((lax.axis_index("x") * 2 + yh) * 2 + core) * IMG_ENC + lax.axis_index("j")
    for x in range(4):
        for rel in range(2):
            for c in range(4):
                base = x * 4 + (yh ^ rel) * 2
                tile = pl.ds(c * 128, 128)
                weight[pl.ds(pl.multiple_of((base + core) * 80, 16), 80), tile] = own[
                    rel, x, c * 80 : (c + 1) * 80, :
                ]
                weight[pl.ds(pl.multiple_of((base + 1 - core) * 80, 16), 80), tile] = other[
                    rel, x, c * 80 : (c + 1) * 80, :
                ]
    rows_out[...] = jnp.zeros(rows_out.shape, jnp.float32)
    for head in range(2):
        for rel in range(2):
            for part, piece in enumerate((own, other)):
                base = head * 128 + (rel * 2 + part) * 32
                lines[...] = piece[rel, half * 2 + head, 320:528, :].astype(jnp.float32)
                for c in range(10):
                    rows_out[base : base + 20, c * 128 : (c + 1) * 128] = lines[
                        pl.ds(c, 20, stride=10), :
                    ]
    row = lax.broadcasted_iota(jnp.int32, (128, VHD), 0)
    column = lax.broadcasted_iota(jnp.int32, (128, VHD), 1)
    wanted = ((row // 32) ^ (yh * 2 + core)) * 20 + row % 32
    order = ((column == wanted) & (row % 32 < 20)).astype(jnp.bfloat16)
    count = jnp.int32(0)
    for i in range(slots.shape[0]):
        count = jnp.where(slots[i] == slot, tokens[i // IMG_ENC, i % IMG_ENC], count)
    rows = [patches[z % 2 * 4 + z // 2].astype(jnp.float32) for z in range(8)]
    normed = rms_scale(jnp.concatenate(rows), gain[...]).astype(jnp.bfloat16)
    qkv = jnp.dot(normed, weight[...], preferred_element_type=jnp.float32)
    flipped = jnp.transpose(qkv).astype(jnp.bfloat16)
    live = lax.broadcasted_iota(jnp.int32, (SLOT, SLOT), 0) < MERGE * count
    for head in range(2):
        base = head * 3 * VHD
        keys = qkv[:, base + VHD : base + 2 * VHD].astype(jnp.bfloat16)
        scores = jnp.dot(
            keys, flipped[base : base + VHD], preferred_element_type=jnp.float32
        ) * (1.0 / math.sqrt(VHD))
        scores = jnp.where(live, scores, NEG)
        weights = jnp.exp(scores - jnp.max(scores, axis=0, keepdims=True))
        denom = jnp.sum(weights, axis=0, keepdims=True)
        attended = jnp.dot(
            flipped[base + 2 * VHD : base + 3 * VHD],
            weights.astype(jnp.bfloat16),
            preferred_element_type=jnp.float32,
        )
        attended = (attended / denom).astype(jnp.bfloat16)
        mixed[head * 128 : (head + 1) * 128, :] = jnp.dot(
            order, attended, preferred_element_type=jnp.float32
        ).astype(jnp.bfloat16)
    partial = lax.dot_general(
        mixed[...],
        rows_out[...].astype(jnp.bfloat16),
        (((0,), (0,)), ((), ())),
        preferred_element_type=jnp.float32,
    ).astype(jnp.bfloat16)
    out[...] = partial.reshape(out.shape)


def norm_kernel(parts, patches, gain, weights, out):
    del weights
    t = lax.axis_index("tp")
    total = patches[t % 2 * 4 + lax.axis_index("h") * 2 + t // 2].astype(jnp.float32)
    for peer in range(8):
        total += parts[peer].astype(jnp.float32)
    total = rms_scale(total, gain[...]).astype(jnp.bfloat16)
    for peer in range(8):
        out[peer] = total


def merge_kernel(rows, own, other, out, merged, weight):
    core, yh = lax.axis_index("core"), lax.axis_index("yh")
    for x in range(4):
        for rel in range(2):
            base = x * 4 + (yh ^ rel) * 2
            weight[pl.ds(pl.multiple_of((base + core) * 320, 16), 320), :] = own[x, rel]
            weight[pl.ds(pl.multiple_of((base + 1 - core) * 320, 16), 320), :] = other[x, rel]
    normed = rows[...].reshape(SLOT, VD).astype(jnp.float32)
    for c in range(VD // 128):
        merged[c] = normed[:, c * 128 : (c + 1) * 128]
    total = jnp.zeros((TOK, HD), jnp.float32)
    for r in range(MERGE):
        part = [merged[c, pl.ds(r, TOK, stride=MERGE), :] for c in range(VD // 128)]
        part = jnp.concatenate(part, axis=1).astype(jnp.bfloat16)
        total += jnp.dot(
            part, weight[r * VD : (r + 1) * VD, :], preferred_element_type=jnp.float32
        )
    total = total.astype(jnp.bfloat16)
    for peer in range(out.shape[0]):
        out[peer] = total


def prompt_index():
    return (lax.axis_index("x") * 2 + lax.axis_index("yh")) * 2 + lax.axis_index("core")


def query_positions():
    seq = lax.axis_index("j") * 2 + lax.axis_index("h")
    return seq * 128 + lax.broadcasted_iota(jnp.int32, (1, GROUP * 128), 1) % 128


def select_kernel(tokens, slots, images, after, out):
    del after
    prompt, plane = prompt_index(), lax.axis_index("j")
    shape = (IMG_TOTAL, images.shape[0] * TOK)
    row = lax.broadcasted_iota(jnp.int32, shape, 0)
    column = lax.broadcasted_iota(jnp.int32, shape, 1)
    wanted = jnp.full(shape, -1, jnp.int32)
    begin = jnp.int32(0)
    for k in range(IMG_ENC):
        slot = slots[prompt * IMG_ENC + k]
        count = tokens[prompt, k]
        enc = slot // IMG_ENC
        place = (enc % 2) * 8 + (enc // 2 % 2) * 4 + enc // 4
        base = jnp.where(slot % IMG_ENC == plane, place * TOK - begin, -FAR)
        inside = (row >= begin) & (row < begin + count)
        wanted = jnp.where(inside, row + base, wanted)
        begin = begin + count
    selector = (column == wanted).astype(jnp.bfloat16)
    packed = jnp.dot(
        selector, images[...].reshape(shape[1], HD), preferred_element_type=jnp.float32
    ).astype(jnp.bfloat16)
    for peer in range(out.shape[0]):
        out[peer] = packed


def text_kernel(blocks, tokens, gaps, queries, cached, *refs):
    if blocks[0] == 0:
        after, out, top_out, sum_out, flipped = refs
    else:
        accum, top_in, sum_in, queries_in, after, out, top_out, sum_out = refs
    del after
    prompt = prompt_index()
    if blocks[0] == 0:
        for g in range(GROUP):
            block = queries[0, :, g * HD : (g + 1) * HD].astype(jnp.float32)
            flipped[:, g * 128 : (g + 1) * 128] = jnp.transpose(block).astype(jnp.bfloat16)
    else:
        flipped = queries_in
    factor = LOG2E / math.sqrt(HD)
    begin = jnp.int32(0)
    spans = []
    for k in range(IMG_ENC):
        begin = begin + gaps[prompt, k]
        spans.append((begin, begin + tokens[prompt, k]))
        begin = begin + tokens[prompt, k]
    if blocks[0] == 0:
        top = jnp.full((1, GROUP * 128), NEG, jnp.float32)
        total = jnp.zeros((1, GROUP * 128), jnp.float32)
        out[...] = jnp.zeros(out.shape, jnp.float32)
    else:
        top, total = top_in[...], sum_in[...]
        out[...] = accum[...]
    query = query_positions()
    for part in blocks:
        if part < 4:
            size = 768
            window = cached[2 * part : 2 * part + 2, 0:384, :].reshape(size, 2 * HD)
        else:
            size = 512
            window = cached[4 * part - 16 : 4 * part - 12, 384:512, :].reshape(size, 2 * HD)
        scores = jnp.dot(window[:, 0:HD], flipped[...], preferred_element_type=jnp.float32)
        if part >= 4:
            position = (part - 4) * size + lax.broadcasted_iota(jnp.int32, (size, 1), 0)
            for low, high in spans:
                position = jnp.where((position >= low) & (position < high), FAR, position)
            scores = jnp.where(position <= query, scores, NEG)
        highest = jnp.maximum(top, jnp.max(scores, axis=0, keepdims=True))
        scale = jnp.exp2((top - highest) * factor)
        weights = jnp.exp2((scores - highest) * factor)
        top = highest
        total = total * scale + jnp.sum(weights, axis=0, keepdims=True)
        out[...] = out[...] * scale + lax.dot_general(
            window[:, HD:],
            weights.astype(jnp.bfloat16),
            (((0,), (0,)), ((), ())),
            preferred_element_type=jnp.float32,
        )
    top_out[...] = top
    sum_out[...] = total


def join_kernel(tokens, gaps, images, flipped, accum, top, total, out):
    prompt = prompt_index()
    factor = LOG2E / math.sqrt(HD)
    keys = (images[0] + images[1]) + (images[2] + images[3])
    values = (images[4] + images[5]) + (images[6] + images[7])
    index = lax.broadcasted_iota(jnp.int32, (IMG_TOTAL, 1), 0)
    position = index
    begin = jnp.int32(0)
    for k in range(IMG_ENC):
        position = position + jnp.where(index >= begin, gaps[prompt, k], 0)
        begin = begin + tokens[prompt, k]
    scores = jnp.dot(keys, flipped[...], preferred_element_type=jnp.float32)
    scores = jnp.where(position <= query_positions(), scores, NEG)
    highest = jnp.maximum(top[...], jnp.max(scores, axis=0, keepdims=True))
    scale = jnp.exp2((top[...] - highest) * factor)
    weights = jnp.exp2((scores - highest) * factor)
    denom = total[...] * scale + jnp.sum(weights, axis=0, keepdims=True)
    joined = accum[...] * scale + lax.dot_general(
        values,
        weights.astype(jnp.bfloat16),
        (((0,), (0,)), ((), ())),
        preferred_element_type=jnp.float32,
    )
    joined = joined / denom
    for g in range(GROUP):
        block = jnp.transpose(joined[:, g * 128 : (g + 1) * 128])
        out[0, :, g * HD : (g + 1) * HD] = block.astype(jnp.bfloat16)


def per_device(
    patches,
    image_tokens,
    image_gap,
    image_slot,
    norm_gain,
    merge_gain,
    w_qkv,
    w_out,
    kv_merge,
    queries,
    text_kv,
    cache_kv,
):
    bf16, f32 = jnp.bfloat16, jnp.float32
    lanes = GROUP * 128

    def after(value, event):
        return lax.optimization_barrier((value, event))[0]

    def swap_x(value, bits):
        return lax.ppermute(value, "x", [(i, i ^ bits) for i in range(4)])

    def call(kernel, name, out_shape, in_specs, scratch=(), cost=(0, 0, 0)):
        return pl.pallas_call(
            kernel,
            out_shape=out_shape,
            in_specs=in_specs,
            out_specs=jax.tree.map(lambda leaf: VMEM, out_shape),
            scratch_shapes=scratch,
            compiler_params=params(),
            cost_estimate=pl.CostEstimate(
                flops=cost[0], bytes_accessed=cost[1], transcendentals=cost[2]
            ),
            name=name,
        )

    def array(shape, dtype=bf16):
        return jax.ShapeDtypeStruct(shape, dtype)

    past = jnp.concatenate([cache_kv[0], text_kv[0]], axis=0)
    past = lax.all_gather(past, SEQ, axis=0)

    heads, sent = pl.pallas_call(
        pack_kernel,
        out_shape=(array((848, 128)), array((8, 32, VD))),
        in_specs=[ANY] * 4,
        out_specs=(VMEM, VMEM),
        scratch_shapes=[
            pltpu.VMEM((80, 960), bf16),
            pltpu.VMEM((20, VD), bf16),
            pltpu.VMEM((320, 256), bf16),
            pltpu.VMEM((4, 32, VD), bf16),
            pltpu.VMEM((208, 128), f32),
            pltpu.SemaphoreType.DMA((4,)),
        ],
        cost_estimate=pl.CostEstimate(flops=1_000_000, bytes_accessed=2_000_000, transcendentals=0),
        name="pack",
    )(w_qkv, w_out, kv_merge, patches)
    mine, theirs = heads, swap(heads, "yh")

    image = lax.all_to_all(sent, SEQ_BACK, 0, 0)
    first = lax.all_gather(mine[0:528], "x", axis=0)
    second = lax.all_gather(theirs[0:528], "x", axis=0)
    own = jnp.stack([first, second])
    other = swap(after(own, image), "core")

    parts = call(
        vision_kernel,
        "vision",
        array((8, 32, VD)),
        [SMEM] * 2 + [VMEM] * 4,
        [
            pltpu.VMEM((VD, 512), bf16),
            pltpu.VMEM((208, 128), f32),
            pltpu.VMEM((256, VD), f32),
            pltpu.VMEM((256, SLOT), bf16),
        ],
        (600_000_000, 5_000_000, 131072),
    )(image_tokens, image_slot, image, norm_gain.reshape(1, VD), own, other)
    merge_pair = after(jnp.stack([mine[528:848], theirs[528:848]]), parts)
    merge_own = lax.all_gather(merge_pair, "x", axis=0)
    parts = lax.all_to_all(parts, ("h", "tp"), 0, 0)

    rows = call(
        norm_kernel, "norm", array((8, 32, VD)), [VMEM] * 3 + [ANY], (), (1_000_000, 2_000_000, 32)
    )(parts, image, merge_gain.reshape(1, VD), merge_own)
    merge_other = swap(after(merge_own, rows), "core")
    rows = lax.all_to_all(rows, ("h", "tp"), 0, 0)

    image_kv = call(
        merge_kernel,
        "merge",
        array((16, TOK, HD)),
        [VMEM] * 3,
        [pltpu.VMEM((VD // 128, SLOT, 128), f32), pltpu.VMEM((MERGE * VD, HD), bf16)],
        (84_000_000, 3_000_000, 0),
    )(rows, merge_own, merge_other)
    every = lax.all_to_all(image_kv, ENC_BACK, 0, 0)

    state = (array((HD, lanes), f32), array((1, lanes), f32), array((1, lanes), f32))
    *state_a, flipped = call(
        functools.partial(text_kernel, (0, 1, 2)),
        "cached",
        state + (array((HD, lanes)),),
        [SMEM] * 2 + [VMEM] * 2 + [ANY],
        (),
        (1_200_000_000, 3_000_000, lanes * 2304),
    )(image_tokens, image_gap, queries, past, image_kv)
    packed = call(
        select_kernel,
        "select",
        array((8, IMG_TOTAL, HD)),
        [SMEM] * 2 + [VMEM, ANY],
        (),
        (42_000_000, 600_000, 0),
    )(image_tokens, image_slot, every, flipped)
    accum, top, total = call(
        functools.partial(text_kernel, (3, 4, 5)),
        "text",
        state,
        [SMEM] * 2 + [VMEM] * 6 + [ANY],
        (),
        (1_000_000_000, 3_000_000, lanes * 1792),
    )(image_tokens, image_gap, queries, past, *state_a, flipped, packed)
    images = lax.all_to_all(packed, SEQ_BACK, 0, 0)

    return call(
        join_kernel,
        "join",
        array((1, 128, lanes)),
        [SMEM] * 2 + [VMEM] * 5,
        (),
        (84_000_000, 2_000_000, lanes * 160),
    )(image_tokens, image_gap, images, flipped, accum, top, total)


def solution(mesh):
    fine = Mesh(
        mesh.devices.reshape(4, 2, 2, 4, 2, 4), ("x", "yh", "core", "j", "h", "tp")
    )
    in_specs = (
        P(ENC, SEQ, None),
        P(),
        P(),
        P(),
        P(),
        P(),
        P(ENC, "tp"),
        P(("tp",) + ENC, None),
        P(ENC, "tp"),
        P(ENC, SEQ, "tp"),
        P(ENC, SEQ, "tp"),
        P(ENC, SEQ, "tp"),
    )
    return jax.shard_map(
        per_device, mesh=fine, in_specs=in_specs, out_specs=P(ENC, SEQ, "tp"), check_vma=False
    )
```
